32 devices in a mesh: parts: 2 (over x), tile: 8 (over z, y), row: 2 (over core).
Axes of the slice: x: 2, y: 2, z: 4, core: 2. Of those that a mesh axis runs over, the one named last changes fastest.
Arguments:
- directions: bfloat16 [256, 32, 384], P(('parts', 'tile')), parts along dimension 0, may hold values from -6 to 6
- sensitivity: bfloat16 [16, 512, 12288], P(('parts', 'tile'), 'row'), parts along dimension 0, may hold values from -0.0546875 to 0.0546875
- data_weight: float32 [16, 512], P(('parts', 'tile'), 'row'), parts along dimension 0, may hold values from 1 to 4
- foot_list: int32 [16, 32], P(('parts', 'tile')), parts along dimension 0, may hold values from 0 to 127, as said below
- foot_mask: int32 [16, 32], P(('parts', 'tile')), parts along dimension 0, may hold values from 0 to 1, as said below
Outputs:
- gradient: float32 [256, 32, 384], P(('parts', 'tile')), parts along dimension 0
The draws below stay inside these ranges and needn't reach their ends.
There are 2 independent parts, one for each index of `parts`. The reference program is written for one: setup_inputs(seed, part) draws one part's arguments, and reference() takes and returns one part's arrays. A program takes and returns all parts, laid end to end along the dimension named above; each array names one. Nothing has to cross between parts.
Inputs may be any that keep to these rules, and one draw needn't show every extreme that they name: `foot_list`: block b belongs to owner b // 16 of the tile axis. Each tile's list names 32 distinct blocks, exactly 4 from each of 8 owners. `foot_mask`: at least three quarters of each tile's entries are live.
All inputs are finite; a program needn't handle non-finite values.
Results may differ from the reference program's by a relative error of at most 0.0028.
Values may be sent and summed in bfloat16 or wider, within the bound.
No kernel may reach another device: no remote copies, remote signals or barrier semaphores. Data moves between devices by JAX's collectives and lax.ppermute only.
A program may use at most 64 MiB of HBM per device.

```python
import math
import jax
import jax.numpy as jnp
from jax import lax

NV = 32
BLK_DEV = 16
FOOT = 32
TILES = 8
ROWS = 512
NBLK = 128
CAP = 4


def draw_foot_list(key, part):
    key = jax.random.fold_in(key, 11)
    first_key, second_key = jax.random.split(key)
    owners_per = FOOT // CAP
    shifted = jax.random.randint(first_key, (TILES,), 0, TILES)
    owner_ids = (jnp.arange(TILES)[:, None] + shifted[:, None] + (jnp.arange(FOOT) // CAP)[None, :]) % TILES
    scores = jax.random.randint(second_key, (TILES, owners_per, BLK_DEV), 0, 1 << 20) * BLK_DEV + jnp.arange(BLK_DEV)
    slot_pick = jnp.argsort(scores, axis=-1)[:, :, :CAP].reshape(TILES, FOOT)
    return (owner_ids * BLK_DEV + slot_pick).astype(jnp.int32)


def draw_foot_mask(key, part):
    key = jax.random.fold_in(key, 12)
    first_key, second_key = jax.random.split(key)
    live_count = jax.random.randint(first_key, (TILES, 1), (3 * FOOT + 3) // 4, FOOT + 1)
    scores = jax.random.randint(second_key, (TILES, FOOT), 0, 1 << 20) * FOOT + jnp.arange(FOOT)
    ranked = jnp.argsort(jnp.argsort(scores, axis=-1), axis=-1)
    return (ranked < live_count).astype(jnp.int32)


def levels(own_key, dims, cuts, low, high):
    level = 1.0
    for dim, shards_of in cuts:
        steps = jax.random.uniform(jax.random.fold_in(jax.random.fold_in(own_key, 6), dim), (shards_of,), jnp.float32, low / len(cuts), high / len(cuts))
        level = level * jnp.repeat(jnp.exp(steps), dims[dim] // shards_of).reshape((-1,) + (1,) * (len(dims) - 1 - dim))
    return level


def gaussian(stream_key, dims, spread, reach, cuts=(), held_as=jnp.bfloat16):
    drawn = spread * jax.random.normal(stream_key, dims, jnp.float32)
    if cuts:
        drawn = drawn * levels(stream_key, dims, cuts, -0.22, 0.18)
    return jnp.clip(drawn, -reach, reach).astype(held_as)


def setup_inputs(seed: int = 0, part: int = 0) -> dict:
    keys = jax.random.split(jax.random.key(seed), 6)
    own_keys = jax.random.split(jax.random.fold_in(keys[5], part), 6)
    return {
        "directions": gaussian(own_keys[0], (NBLK, NV, 384), 1.0, 6.0, ((0, 8),)),
        "sensitivity": gaussian(own_keys[1], (TILES, ROWS, FOOT * 384), (FOOT * 384) ** -0.5, 0.0546875, ((0, 8), (1, 2))),
        "data_weight": jnp.clip(jnp.exp(math.log(4.0) - 1.3862944 * jax.random.uniform(own_keys[2], (TILES, ROWS), jnp.float32) ** levels(own_keys[2], (TILES, ROWS), ((0, 8), (1, 2)), -0.2, 0.2)), 1.0, 4.0),
        "foot_list": draw_foot_list(jax.random.fold_in(jax.random.fold_in(keys[5], part), 71), part),
        "foot_mask": draw_foot_mask(jax.random.fold_in(jax.random.fold_in(keys[5], part), 71), part),
    }


def reference(directions, sensitivity, data_weight, foot_list, foot_mask):
    def one_tile(inputs):
        sens_rows, weights, block_ids, live = inputs
        picked = directions[block_ids] * live.astype(directions.dtype)[:, None, None]
        flat_dirs = picked.transpose(1, 0, 2).reshape(NV, FOOT * 384)
        predicted = jnp.dot(sens_rows, flat_dirs.T, preferred_element_type=jnp.float32)
        scaled = ((weights * weights)[:, None] * predicted).astype(jnp.bfloat16)
        summed = jnp.dot(scaled.T, sens_rows, preferred_element_type=jnp.float32)
        result = summed.reshape(NV, FOOT, 384).transpose(1, 0, 2)
        return result * live.astype(jnp.float32)[:, None, None]

    foot_grads = lax.map(one_tile, (sensitivity, data_weight, foot_list, foot_mask))
    gradient = jnp.zeros((NBLK, NV, 384), jnp.float32)
    gradient = gradient.at[foot_list.reshape(-1)].add(foot_grads.reshape(TILES * FOOT, NV, 384))
    return gradient
```

```python
import functools

import jax
import jax.numpy as jnp
from jax import lax
from jax.experimental import pallas as pl
from jax.experimental.pallas import tpu as pltpu
from jax.sharding import PartitionSpec as P

VMEM = pl.BlockSpec(memory_space=pltpu.VMEM)
SMEM = pl.BlockSpec(memory_space=pltpu.SMEM)
ANY = pl.BlockSpec(memory_space=pl.ANY)
PARAMS = pltpu.CompilerParams(vmem_limit_bytes=40 << 20)


def swap_rows(x):
    return lax.ppermute(x, "row", [(0, 1), (1, 0)])


def exchange(x, step):
    tiles = lax.axis_size("tile")
    pairs = [(2 * t + r, 2 * (t ^ (2 * step + r)) + r) for t in range(tiles) for r in range(2)]
    return lax.ppermute(x, ("tile", "row"), pairs)


def select_kernel(steps, capacity, here_ref, *refs):
    lists, dirs_ref = refs[:steps], refs[steps]
    outs, chosen_ref = refs[steps + 1 : 2 * steps + 1], refs[2 * steps + 1]
    slots_ref = refs[2 * steps + 2]
    blocks = dirs_ref.shape[0]
    tile = here_ref[0]
    for p in range(steps):
        count = jnp.int32(0)
        for k in range(lists[p].shape[1]):
            block = lists[p][0, k]
            mine = lax.div(block, blocks) == tile
            slots_ref[jnp.where(mine, count, capacity)] = lax.rem(block, blocks)
            count = count + mine.astype(jnp.int32)
        for c in range(capacity):
            block = slots_ref[c]
            chosen_ref[p * capacity + c] = block
            outs[p][c] = dirs_ref[block]


def find_columns(steps, capacity, blocks, here_ref, list_ref, count_ref, column_ref):
    tile, core = here_ref[0], here_ref[1]
    for p in range(steps):
        count_ref[p] = 0
    for k in range(list_ref.shape[1]):
        apart = lax.div(list_ref[0, k], blocks) ^ tile
        step = lax.div(apart, 2)
        mine = lax.rem(apart, 2) == core
        count = count_ref[step]
        column_ref[jnp.where(mine, step * capacity + count, steps * capacity)] = k
        count_ref[step] = count + mine.astype(jnp.int32)


def column_copies(slots, capacity, width, column_ref, sens_refs, held_ref, sems):
    copies = []
    rows = sens_refs[0].shape[0]
    for place, slot in enumerate(slots):
        start = pl.multiple_of(column_ref[slot] * width, 128)
        for half in range(2):
            copies.append(
                pltpu.make_async_copy(
                    sens_refs[half].at[:, pl.ds(start, width)],
                    held_ref.at[pl.ds(half * rows, rows), pl.ds(place * width, width)],
                    sems.at[2 * place + half],
                )
            )
    return copies


def predict_kernel(
    steps, capacity, blocks, here_ref, list_ref, mask_ref, own_ref, other_ref, *refs
):
    dirs = refs[:steps]
    out_ref, count_ref, column_ref, held_ref, flat_ref, sems = refs[steps:]
    vecs, width = dirs[0].shape[1:]
    rows = own_ref.shape[0]
    find_columns(steps, capacity, blocks, here_ref, list_ref, count_ref, column_ref)
    order = [p * capacity + c for p in range(steps) for c in range(capacity)]
    copies = column_copies(order, capacity, width, column_ref, (own_ref, other_ref), held_ref, sems)
    for copy in copies:
        copy.start()
    for p in range(steps):
        for c in range(capacity):
            slot = p * capacity + c
            live = mask_ref[0, column_ref[slot]].astype(jnp.float32)
            block = dirs[p][c].astype(jnp.float32) * live
            flat_ref[:, slot * width : (slot + 1) * width] = block.astype(jnp.bfloat16)
    total = jnp.zeros((vecs, 2 * rows), jnp.float32)
    for p in range(steps):
        for copy in copies[2 * p * capacity : 2 * (p + 1) * capacity]:
            copy.wait()
        span = slice(p * capacity * width, (p + 1) * capacity * width)
        total += lax.dot_general(
            flat_ref[:, span],
            held_ref[:, span],
            (((1,), (1,)), ((), ())),
            preferred_element_type=jnp.float32,
        )
    out_ref[0] = total[:, :rows]
    out_ref[1] = total[:, rows:]


def back_kernel(
    group, steps, capacity, blocks, here_ref, list_ref, mask_ref, own_ref, other_ref, *refs
):
    mine_ref, theirs_ref, own_weight_ref, other_weight_ref = refs[:4]
    outs = refs[4 : 4 + len(group)]
    count_ref, column_ref, held_ref, sems = refs[4 + len(group) :]
    width = outs[0].shape[2]
    find_columns(steps, capacity, blocks, here_ref, list_ref, count_ref, column_ref)
    order = [p * capacity + c for p in group for c in range(capacity)]
    copies = column_copies(order, capacity, width, column_ref, (own_ref, other_ref), held_ref, sems)
    for copy in copies:
        copy.start()
    own_weight, other_weight = own_weight_ref[...], other_weight_ref[...]
    scaled = jnp.concatenate(
        [
            (own_weight * own_weight) * (mine_ref[0] + theirs_ref[1]),
            (other_weight * other_weight) * (mine_ref[1] + theirs_ref[0]),
        ],
        axis=1,
    ).astype(jnp.bfloat16)
    for place, p in enumerate(group):
        for copy in copies[2 * place * capacity : 2 * (place + 1) * capacity]:
            copy.wait()
        span = slice(place * capacity * width, (place + 1) * capacity * width)
        grads = jnp.dot(scaled, held_ref[:, span], preferred_element_type=jnp.float32)
        for c in range(capacity):
            live = mask_ref[0, column_ref[p * capacity + c]].astype(jnp.float32)
            part = grads[:, c * width : (c + 1) * width] * live
            outs[place][c] = part.astype(jnp.bfloat16)


def sum_kernel(steps, capacity, own_chosen_ref, other_chosen_ref, *refs):
    own, other = refs[:steps], refs[steps : 2 * steps]
    out_ref, held_ref = refs[2 * steps :]
    out_ref[...] = jnp.zeros_like(out_ref)
    held_ref[...] = jnp.zeros_like(held_ref)
    for chosen_ref, chunks, total_ref in (
        (own_chosen_ref, own, out_ref),
        (other_chosen_ref, other, held_ref),
    ):
        for p in range(steps):
            for c in range(capacity):
                total_ref[chosen_ref[p * capacity + c]] += chunks[p][c].astype(jnp.float32)
    out_ref[...] += held_ref[...]


def on_device(directions, sensitivity, data_weight, foot_list, foot_mask):
    tiles = lax.axis_size("tile")
    blocks, vecs, width = directions.shape
    rows = sensitivity.shape[1]
    foot = foot_list.shape[1]
    steps, capacity = tiles // 2, foot // tiles
    here = jnp.stack([lax.axis_index("tile"), lax.axis_index("row")]).astype(jnp.int32)
    far_first = list(reversed(range(steps)))

    own_sens = sensitivity[0]
    other_sens = swap_rows(own_sens)
    other_weight = swap_rows(data_weight)
    lists = {p: exchange(foot_list, p) for p in far_first}

    chunk = jax.ShapeDtypeStruct((capacity, vecs, width), jnp.bfloat16)
    *chunks, chosen = pl.pallas_call(
        functools.partial(select_kernel, steps, capacity),
        out_shape=[chunk] * steps + [jax.ShapeDtypeStruct((steps * capacity,), jnp.int32)],
        in_specs=[SMEM] * (steps + 1) + [VMEM],
        out_specs=[VMEM] * steps + [SMEM],
        scratch_shapes=[pltpu.SMEM((capacity + 1,), jnp.int32)],
        compiler_params=PARAMS,
        name="select_blocks",
    )(here, *[lists[p] for p in range(steps)], directions)
    fetched = {p: exchange(chunks[p], p) for p in far_first}
    other_chosen = swap_rows(chosen)

    span = steps * capacity * width
    partial = pl.pallas_call(
        functools.partial(predict_kernel, steps, capacity, blocks),
        out_shape=jax.ShapeDtypeStruct((2, vecs, rows), jnp.float32),
        in_specs=[SMEM] * 3 + [ANY] * 2 + [VMEM] * steps,
        out_specs=VMEM,
        scratch_shapes=[
            pltpu.SMEM((steps,), jnp.int32),
            pltpu.SMEM((steps * capacity + 1,), jnp.int32),
            pltpu.VMEM((2 * rows, span), jnp.bfloat16),
            pltpu.VMEM((vecs, span), jnp.bfloat16),
            pltpu.SemaphoreType.DMA((2 * steps * capacity,)),
        ],
        compiler_params=PARAMS,
        name="predict",
    )(here, foot_list, foot_mask, own_sens, other_sens, *[fetched[p] for p in range(steps)])
    other_partial = swap_rows(partial)

    half = (steps + 1) // 2
    returned = {}
    for group in (far_first[:half], far_first[half:]):
        grads = pl.pallas_call(
            functools.partial(back_kernel, group, steps, capacity, blocks),
            out_shape=[chunk] * len(group),
            in_specs=[SMEM] * 3 + [ANY] * 2 + [VMEM] * 4,
            out_specs=[VMEM] * len(group),
            scratch_shapes=[
                pltpu.SMEM((steps,), jnp.int32),
                pltpu.SMEM((steps * capacity + 1,), jnp.int32),
                pltpu.VMEM((2 * rows, len(group) * capacity * width), jnp.bfloat16),
                pltpu.SemaphoreType.DMA((2 * len(group) * capacity,)),
            ],
            compiler_params=PARAMS,
            name="back_project",
        )(
            here, foot_list, foot_mask, own_sens, other_sens,
            partial, other_partial, data_weight, other_weight,
        )
        for place, p in enumerate(group):
            returned[p] = exchange(grads[place], p)
    other_returned = {p: swap_rows(returned[p]) for p in far_first}

    return pl.pallas_call(
        functools.partial(sum_kernel, steps, capacity),
        out_shape=jax.ShapeDtypeStruct((blocks, vecs, width), jnp.float32),
        in_specs=[SMEM] * 2 + [VMEM] * (2 * steps),
        out_specs=VMEM,
        scratch_shapes=[pltpu.VMEM((blocks, vecs, width), jnp.float32)],
        compiler_params=PARAMS,
        name="sum_blocks",
    )(
        chosen, other_chosen,
        *[returned[p] for p in range(steps)], *[other_returned[p] for p in range(steps)],
    )


def solution(mesh):
    in_specs = (
        P(("parts", "tile"), None, None),
        P(("parts", "tile"), "row", None),
        P(("parts", "tile"), "row"),
        P(("parts", "tile"), None),
        P(("parts", "tile"), None),
    )
    out_specs = P(("parts", "tile"), None, None)
    return jax.shard_map(
        on_device, mesh=mesh, in_specs=in_specs, out_specs=out_specs, check_vma=False
    )
```

```python
import functools

import jax
import jax.numpy as jnp
from jax import lax
from jax.experimental import pallas as pl
from jax.experimental.pallas import tpu as pltpu
from jax.sharding import PartitionSpec as P

VMEM = pl.BlockSpec(memory_space=pltpu.VMEM)
SMEM = pl.BlockSpec(memory_space=pltpu.SMEM)
HBM = pl.BlockSpec(memory_space=pltpu.HBM)
PARAMS = pltpu.CompilerParams(vmem_limit_bytes=32 << 20)


def swap_rows(x):
    return lax.ppermute(x, "row", [(0, 1), (1, 0)])


def exchange(x, step):
    tiles = lax.axis_size("tile")
    pairs = [(2 * t + r, 2 * (t ^ (2 * step + r)) + r) for t in range(tiles) for r in range(2)]
    return lax.ppermute(x, ("tile", "row"), pairs)


def in_hbm(x):
    return pltpu.with_memory_space_constraint(x, pltpu.HBM)


def cost(moved, flops=0):
    return pl.CostEstimate(flops=flops, bytes_accessed=moved, transcendentals=0)


def plan_kernel(steps, capacity, here_ref, list_ref, mask_ref, dirs_ref, *refs):
    column_ref, live_ref, held_dirs_ref, held_list_ref, held_mask_ref, count_ref, sems = refs
    slots, blocks = steps * capacity, dirs_ref.shape[0]
    pairs = [(list_ref, held_list_ref), (mask_ref, held_mask_ref), (dirs_ref, held_dirs_ref)]
    copies = [pltpu.make_async_copy(*pair, sems.at[i]) for i, pair in enumerate(pairs)]
    for copy in copies:
        copy.start()
    for s in range(2 * steps):
        count_ref[s] = 0
    for copy in copies[:2]:
        copy.wait()
    tile, core = here_ref[0], here_ref[1]
    for k in range(list_ref.shape[1]):
        apart = lax.div(held_list_ref[0, k], blocks) ^ tile
        count = count_ref[apart]
        count_ref[apart] = count + 1
        mine = (apart & 1) == core
        slot = jnp.where(mine, (apart >> 1) * capacity + count, slots)
        column_ref[slot] = k
        live_ref[slot] = held_mask_ref[0, k]
    copies[2].wait()


def stage_kernel(slots, column_ref, own_ref, other_ref, own_out_ref, other_out_ref, sems):
    width = own_out_ref.shape[1] // slots
    copies = []
    for slot in range(slots):
        start = pl.multiple_of(column_ref[slot] * width, 128)
        for half, (sens_ref, out_ref) in enumerate(
            ((own_ref, own_out_ref), (other_ref, other_out_ref))
        ):
            copies.append(
                pltpu.make_async_copy(
                    sens_ref.at[:, pl.ds(start, width)],
                    out_ref.at[:, pl.ds(slot * width, width)],
                    sems.at[2 * slot + half],
                )
            )
            copies[-1].start()
    for copy in copies:
        copy.wait()


def select_kernel(steps, capacity, here_ref, *refs):
    lists, dirs_ref = refs[:steps][::-1], refs[steps]
    outs, (chosen_ref, slots_ref) = refs[steps + 1 : 2 * steps + 1], refs[2 * steps + 1 :]
    blocks = dirs_ref.shape[0]
    first = here_ref[0] * blocks
    for p in range(steps):
        found = jnp.int32(0)
        for k in range(lists[p].shape[1]):
            block = lists[p][0, k] - first
            mine = (block >= 0) & (block < blocks)
            slots_ref[jnp.where(mine, found, capacity)] = block
            found = found + mine.astype(jnp.int32)
        for c in range(capacity):
            block = slots_ref[c]
            chosen_ref[p * capacity + c] = block
            outs[p][c] = dirs_ref[block]


def predict_kernel(order, capacity, live_ref, own_ref, other_ref, weight_ref, *refs):
    dirs, (out_ref, flat_ref) = refs[: len(order)], refs[len(order) :]
    vecs, width = dirs[0].shape[1:]
    size = capacity * width
    for chunk_ref, p in zip(dirs, order):
        for c in range(capacity):
            live = live_ref[p * capacity + c].astype(jnp.float32)
            block = chunk_ref[c].astype(jnp.float32) * live
            start = p * size + c * width
            flat_ref[:, start : start + width] = block.astype(jnp.bfloat16)
    weight = weight_ref[...]
    for half, sens_ref in enumerate((own_ref, other_ref)):
        out_ref[half, :vecs] = lax.dot_general(
            flat_ref[...],
            sens_ref[...],
            (((1,), (1,)), ((), ())),
            preferred_element_type=jnp.float32,
        )
        out_ref[half, vecs:] = jnp.broadcast_to(weight * weight, (8, weight.shape[1]))


def back_kernel(group, capacity, live_ref, own_ref, other_ref, mine_ref, theirs_ref, *outs):
    vecs, width = outs[0].shape[1:]
    own = mine_ref[0, vecs : vecs + 1] * (mine_ref[0, :vecs] + theirs_ref[1, :vecs])
    other = theirs_ref[0, vecs : vecs + 1] * (mine_ref[1, :vecs] + theirs_ref[0, :vecs])
    own, other = own.astype(jnp.bfloat16), other.astype(jnp.bfloat16)
    size = capacity * width
    for place, slot in enumerate(group):
        span = slice(slot * size, (slot + 1) * size)
        grads = jnp.dot(own, own_ref[:, span], preferred_element_type=jnp.float32)
        grads += jnp.dot(other, other_ref[:, span], preferred_element_type=jnp.float32)
        for c in range(capacity):
            live = live_ref[slot * capacity + c].astype(jnp.float32)
            part = grads[:, c * width : (c + 1) * width] * live
            outs[place][c] = part.astype(jnp.bfloat16)


def add_chunk(capacity, chosen_ref, slot, chunk_ref, total_ref):
    for c in range(capacity):
        total_ref[chosen_ref[slot * capacity + c]] += chunk_ref[c].astype(jnp.float32)


def sum_kernel(order, capacity, chosen_ref, *refs):
    out_ref = refs[-1]
    out_ref[...] = jnp.zeros_like(out_ref)
    for slot, chunk_ref in zip(order, refs):
        add_chunk(capacity, chosen_ref, slot, chunk_ref, out_ref)


def finish_kernel(order, capacity, chosen_ref, own_ref, *refs):
    sum_kernel(order, capacity, chosen_ref, *refs)
    refs[-1][...] += own_ref[...]


def on_device(directions, sensitivity, data_weight, foot_list, foot_mask):
    tiles = lax.axis_size("tile")
    blocks, vecs, width = directions.shape
    rows = sensitivity.shape[1]
    foot = foot_list.shape[1]
    steps, capacity = tiles // 2, foot // tiles
    slots = steps * capacity
    here = jnp.stack([lax.axis_index("tile"), lax.axis_index("row")]).astype(jnp.int32)
    half = (steps + 1) // 2
    far, near = list(range(half, steps)), list(range(half))
    order = far + near

    own_sens = in_hbm(sensitivity[0])
    other_sens = in_hbm(swap_rows(sensitivity[0]))
    lists = {p: exchange(foot_list, p) for p in order}
    table = jax.ShapeDtypeStruct((slots + 1,), jnp.int32)
    column, live, held_dirs = pl.pallas_call(
        functools.partial(plan_kernel, steps, capacity),
        out_shape=[table, table, pltpu.VMEM(directions.shape, jnp.bfloat16)],
        in_specs=[SMEM] + [HBM] * 3,
        out_specs=[SMEM] * 2 + [VMEM],
        scratch_shapes=[
            pltpu.SMEM(foot_list.shape, jnp.int32),
            pltpu.SMEM(foot_mask.shape, jnp.int32),
            pltpu.SMEM((tiles,), jnp.int32),
            pltpu.SemaphoreType.DMA((3,)),
        ],
        compiler_params=PARAMS,
        cost_estimate=cost(1),
        name="plan_columns",
    )(here, in_hbm(foot_list), in_hbm(foot_mask), in_hbm(directions))

    chunk = jax.ShapeDtypeStruct((capacity, vecs, width), jnp.bfloat16)
    *chunks, chosen = pl.pallas_call(
        functools.partial(select_kernel, steps, capacity),
        out_shape=[chunk] * steps + [jax.ShapeDtypeStruct((slots,), jnp.int32)],
        in_specs=[SMEM] * (steps + 1) + [VMEM],
        out_specs=[VMEM] * steps + [SMEM],
        scratch_shapes=[pltpu.SMEM((capacity + 1,), jnp.int32)],
        compiler_params=PARAMS,
        cost_estimate=cost(1),
        name="select_blocks",
    )(here, *[lists[p] for p in reversed(range(steps))], held_dirs)
    fetched = {p: exchange(chunks[p], p) for p in order}

    columns = pltpu.VMEM((rows, slots * width), jnp.bfloat16)
    own_sens, other_sens = pl.pallas_call(
        functools.partial(stage_kernel, slots),
        out_shape=[columns] * 2,
        in_specs=[SMEM] + [HBM] * 2,
        out_specs=[VMEM] * 2,
        scratch_shapes=[pltpu.SemaphoreType.DMA((2 * slots,))],
        compiler_params=PARAMS,
        cost_estimate=cost(1),
        name="stage_columns",
    )(column, own_sens, other_sens)

    partial = pl.pallas_call(
        functools.partial(predict_kernel, order, capacity),
        out_shape=jax.ShapeDtypeStruct((2, vecs + 8, rows), jnp.float32),
        in_specs=[SMEM] + [VMEM] * (3 + steps),
        out_specs=VMEM,
        scratch_shapes=[pltpu.VMEM((vecs, slots * width), jnp.bfloat16)],
        compiler_params=PARAMS,
        cost_estimate=cost(1),
        name="predict",
    )(live, own_sens, other_sens, data_weight, *[fetched[p] for p in order])
    partial, chosen = lax.optimization_barrier((partial, chosen))
    other_partial, other_chosen = lax.optimization_barrier((swap_rows(partial), swap_rows(chosen)))

    def back(group, mine):
        return pl.pallas_call(
            functools.partial(back_kernel, group, capacity),
            out_shape=[chunk] * len(group),
            in_specs=[SMEM] + [VMEM] * 4,
            out_specs=[VMEM] * len(group),
            compiler_params=PARAMS,
            cost_estimate=cost(1),
            name="back_project",
        )(live, own_sens, other_sens, mine, other_partial)

    grads = back(order, partial)
    returned = {p: exchange(x, p) for p, x in zip(order, grads)}
    other_returned = {p: swap_rows(returned[p]) for p in order}

    total = jax.ShapeDtypeStruct((blocks, vecs, width), jnp.float32)
    own_sum = pl.pallas_call(
        functools.partial(sum_kernel, order, capacity),
        out_shape=total,
        in_specs=[SMEM] + [VMEM] * len(order),
        out_specs=VMEM,
        compiler_params=PARAMS,
        cost_estimate=cost(1),
        name="sum_blocks",
    )(chosen, *[returned[slot] for slot in order])
    return pl.pallas_call(
        functools.partial(finish_kernel, order, capacity),
        out_shape=total,
        in_specs=[SMEM] + [VMEM] * (1 + len(order)),
        out_specs=VMEM,
        compiler_params=PARAMS,
        cost_estimate=cost(1),
        name="finish_blocks",
    )(other_chosen, own_sum, *[other_returned[slot] for slot in order])


def solution(mesh):
    in_specs = (
        P(("parts", "tile"), None, None),
        P(("parts", "tile"), "row", None),
        P(("parts", "tile"), "row"),
        P(("parts", "tile"), None),
        P(("parts", "tile"), None),
    )
    out_specs = P(("parts", "tile"), None, None)
    return jax.shard_map(
        on_device, mesh=mesh, in_specs=in_specs, out_specs=out_specs, check_vma=False
    )
```

```python
import functools

import jax
import jax.numpy as jnp
from jax import lax
from jax.experimental import pallas as pl
from jax.experimental.pallas import tpu as pltpu
from jax.sharding import PartitionSpec as P

VMEM = pl.BlockSpec(memory_space=pltpu.VMEM)
SMEM = pl.BlockSpec(memory_space=pltpu.SMEM)
HBM = pl.BlockSpec(memory_space=pltpu.HBM)
ANY = pl.BlockSpec(memory_space=pl.ANY)
PARAMS = pltpu.CompilerParams(vmem_limit_bytes=32 << 20)


def swap_rows(x):
    return lax.ppermute(x, "row", [(0, 1), (1, 0)])


def exchange(x, apart):
    tiles = lax.axis_size("tile")
    pairs = [(2 * t + r, 2 * (t ^ apart[r]) + r) for t in range(tiles) for r in apart]
    return lax.ppermute(x, ("tile", "row"), pairs)


def in_hbm(x):
    return pltpu.with_memory_space_constraint(x, pltpu.HBM)


def cost(moved, flops=0):
    return pl.CostEstimate(flops=flops, bytes_accessed=moved, transcendentals=0)


def column_copies(slots, column_ref, sens_ref, out_ref, sems):
    width = out_ref.shape[1] // slots
    copies = []
    for slot in range(slots):
        start = pl.multiple_of(column_ref[slot] * width, 128)
        copies.append(
            pltpu.make_async_copy(
                sens_ref.at[:, pl.ds(start, width)],
                out_ref.at[:, pl.ds(slot * width, width)],
                sems.at[slot],
            )
        )
        copies[-1].start()
    return copies


def find_asked(list_ref, owner, blocks, slot, ids_ref):
    first, spare = owner * blocks, ids_ref.shape[0] - 1
    for k in range(list_ref.shape[1]):
        block = list_ref[0, k] - first
        mine = (block >= 0) & (block < blocks)
        ids_ref[jnp.where(mine, slot, spare)] = block
        slot = slot + mine.astype(jnp.int32)


def plan_kernel(tiles, capacity, blocks, here_ref, list_ref, mask_ref, sens_ref, *refs):
    column_ref, live_ref, own_ids_ref, out_ref = refs[:4]
    held_list_ref, held_mask_ref, count_ref, sems = refs[4:]
    steps = tiles // 2
    slots = steps * capacity
    pairs = [(list_ref, held_list_ref), (mask_ref, held_mask_ref)]
    copies = [pltpu.make_async_copy(*pair, sems.at[slots + i]) for i, pair in enumerate(pairs)]
    for copy in copies:
        copy.start()
    for s in range(tiles):
        count_ref[s] = 0
    for copy in copies:
        copy.wait()
    tile, core = here_ref[0], here_ref[1]
    mirror = tile ^ (tiles - 2)
    seen_from = jnp.where(core == 0, tile, mirror)
    for k in range(list_ref.shape[1]):
        apart = lax.div(held_list_ref[0, k], blocks) ^ seen_from
        count = count_ref[apart]
        count_ref[apart] = count + 1
        slot = (steps - 1 - apart) * capacity + count
        slot = jnp.where(apart < steps, slot, slots)
        column_ref[slot] = k
        live_ref[slot] = held_mask_ref[0, k]
    copies = column_copies(slots, column_ref, sens_ref, out_ref, sems)
    find_asked(held_list_ref, tile, blocks, 0, own_ids_ref)
    find_asked(held_list_ref, mirror, blocks, capacity, own_ids_ref)
    for copy in copies:
        copy.wait()


def stage_kernel(slots, column_ref, sens_ref, out_ref, sems):
    for copy in column_copies(slots, column_ref, sens_ref, out_ref, sems):
        copy.wait()


def search_kernel(tiles, capacity, blocks, here_ref, own_ids_ref, *refs):
    *lists, ids_ref = refs
    steps, tile = tiles // 2, here_ref[0]
    slots = steps * capacity
    for part, owner in enumerate((tile, tile ^ (tiles - 2))):
        for turn, list_ref in enumerate(lists):
            find_asked(list_ref, owner, blocks, part * slots + turn * capacity, ids_ref)
        for c in range(capacity):
            ids_ref[part * slots + (steps - 1) * capacity + c] = own_ids_ref[part * capacity + c]


def select_kernel(capacity, here_ref, ids_ref, own_ref, mirror_ref, *refs):
    *outs, dirs_ref, sem = refs
    core = here_ref[1]

    @pl.when(core == 0)
    def _():
        pltpu.make_async_copy(own_ref, dirs_ref, sem.at[0]).start()

    @pl.when(core != 0)
    def _():
        pltpu.make_async_copy(mirror_ref, dirs_ref, sem.at[0]).start()

    pltpu.make_async_copy(own_ref, dirs_ref, sem.at[0]).wait()
    start = core * (len(outs) * capacity)
    for turn, out_ref in enumerate(outs):
        for c in range(capacity):
            out_ref[c] = dirs_ref[ids_ref[start + turn * capacity + c]]


def predict_kernel(capacity, live_ref, own_ref, other_ref, weight_ref, *refs):
    *chunks, out_ref, flat_ref = refs
    vecs, width = chunks[0].shape[1:]
    for turn, chunk_ref in enumerate(chunks):
        for c in range(capacity):
            slot = turn * capacity + c
            live = live_ref[slot].astype(jnp.float32)
            block = chunk_ref[c].astype(jnp.float32) * live
            flat_ref[:, slot * width : (slot + 1) * width] = block.astype(jnp.bfloat16)
    weight = weight_ref[...]
    for side, sens_ref in enumerate((own_ref, other_ref)):
        product = lax.dot_general(
            sens_ref[...],
            flat_ref[...],
            (((1,), (1,)), ((), ())),
            preferred_element_type=jnp.float32,
        )
        out_ref[side, :vecs] = product.T
        out_ref[side, vecs:] = jnp.broadcast_to(weight * weight, (8, weight.shape[1]))


def back_kernel(capacity, live_ref, own_ref, other_ref, mine_ref, theirs_ref, *outs):
    vecs, width = outs[0].shape[1:]
    own = mine_ref[0, vecs : vecs + 1] * (mine_ref[0, :vecs] + theirs_ref[1, :vecs])
    other = theirs_ref[0, vecs : vecs + 1] * (mine_ref[1, :vecs] + theirs_ref[0, :vecs])
    own, other = own.astype(jnp.bfloat16), other.astype(jnp.bfloat16)
    for turn, out_ref in enumerate(outs):
        span = slice(turn * capacity * width, (turn + 1) * capacity * width)
        grads = jnp.dot(own, own_ref[:, span], preferred_element_type=jnp.float32)
        grads += jnp.dot(other, other_ref[:, span], preferred_element_type=jnp.float32)
        for c in range(capacity):
            live = live_ref[turn * capacity + c].astype(jnp.float32)
            part = grads[:, c * width : (c + 1) * width] * live
            out_ref[c] = part.astype(jnp.bfloat16)


def add_chunks(capacity, places, chunks, out_ref):
    out_ref[...] = jnp.zeros_like(out_ref)
    for turn, chunk_ref in enumerate(chunks):
        for c in range(capacity):
            out_ref[places(turn * capacity + c)] += chunk_ref[c].astype(jnp.float32)


def sum_kernel(capacity, here_ref, near_ref, far_ref, *refs):
    *chunks, out_ref = refs
    core, slots = here_ref[1], len(chunks) * capacity
    add_chunks(
        capacity,
        lambda slot: jnp.where(core == 0, near_ref[slot], far_ref[slots + slot]),
        chunks,
        out_ref,
    )


def finish_kernel(capacity, here_ref, near_ref, far_ref, own_ref, *refs):
    *chunks, out_ref = refs
    core, slots = here_ref[1], len(chunks) * capacity
    add_chunks(
        capacity,
        lambda slot: jnp.where(core == 0, far_ref[slots + slot], near_ref[slot]),
        chunks,
        out_ref,
    )
    out_ref[...] += own_ref[...]


def on_device(directions, sensitivity, data_weight, foot_list, foot_mask):
    tiles = lax.axis_size("tile")
    blocks, vecs, width = directions.shape
    rows = sensitivity.shape[1]
    foot = foot_list.shape[1]
    steps, capacity = tiles // 2, foot // tiles
    slots, mirror = steps * capacity, tiles - 2
    here = jnp.stack([lax.axis_index("tile"), lax.axis_index("row")]).astype(jnp.int32)
    order = list(reversed(range(steps)))

    own_sens = in_hbm(sensitivity[0])
    other_sens = in_hbm(swap_rows(sensitivity[0]))
    mirrored = exchange(directions, {1: mirror})
    lists = [exchange(foot_list, {0: s, 1: s}) for s in order[:-1]]

    table = jax.ShapeDtypeStruct((slots + 1,), jnp.int32)
    columns = pltpu.VMEM((rows, slots * width), jnp.bfloat16)
    column, live, own_ids, own_sens = pl.pallas_call(
        functools.partial(plan_kernel, tiles, capacity, blocks),
        out_shape=[table] * 2 + [jax.ShapeDtypeStruct((2 * capacity + 1,), jnp.int32), columns],
        in_specs=[SMEM] + [HBM] * 3,
        out_specs=[SMEM] * 3 + [VMEM],
        scratch_shapes=[
            pltpu.SMEM(foot_list.shape, jnp.int32),
            pltpu.SMEM(foot_mask.shape, jnp.int32),
            pltpu.SMEM((tiles,), jnp.int32),
            pltpu.SemaphoreType.DMA((slots + 2,)),
        ],
        compiler_params=PARAMS,
        cost_estimate=cost(1),
        name="plan_columns",
    )(here, in_hbm(foot_list), in_hbm(foot_mask), own_sens)

    chunk = jax.ShapeDtypeStruct((capacity, vecs, width), jnp.bfloat16)
    ids = pl.pallas_call(
        functools.partial(search_kernel, tiles, capacity, blocks),
        out_shape=jax.ShapeDtypeStruct((2 * slots + 1,), jnp.int32),
        in_specs=[SMEM] * (1 + steps),
        out_specs=SMEM,
        compiler_params=PARAMS,
        cost_estimate=cost(1),
        name="search_lists",
    )(here, own_ids, *lists)
    chunks = pl.pallas_call(
        functools.partial(select_kernel, capacity),
        out_shape=[chunk] * steps,
        in_specs=[SMEM] * 2 + [HBM, ANY],
        out_specs=[VMEM] * steps,
        scratch_shapes=[
            pltpu.VMEM(directions.shape, jnp.bfloat16),
            pltpu.SemaphoreType.DMA((1,)),
        ],
        compiler_params=PARAMS,
        cost_estimate=cost(1),
        name="select_blocks",
    )(here, ids, in_hbm(directions), mirrored)
    fetched = [exchange(x, {0: s, 1: s}) for s, x in zip(order[:-1], chunks)] + [chunks[-1]]

    other_sens = pl.pallas_call(
        functools.partial(stage_kernel, slots),
        out_shape=columns,
        in_specs=[SMEM, HBM],
        out_specs=VMEM,
        scratch_shapes=[pltpu.SemaphoreType.DMA((slots,))],
        compiler_params=PARAMS,
        cost_estimate=cost(1),
        name="stage_columns",
    )(column, other_sens)

    partial = pl.pallas_call(
        functools.partial(predict_kernel, capacity),
        out_shape=jax.ShapeDtypeStruct((2, vecs + 8, rows), jnp.float32),
        in_specs=[SMEM] + [VMEM] * (3 + steps),
        out_specs=VMEM,
        scratch_shapes=[pltpu.VMEM((vecs, slots * width), jnp.bfloat16)],
        compiler_params=PARAMS,
        cost_estimate=cost(1),
        name="predict",
    )(live, own_sens, other_sens, data_weight, *fetched)
    other_partial = swap_rows(partial)

    grads = pl.pallas_call(
        functools.partial(back_kernel, capacity),
        out_shape=[chunk] * steps,
        in_specs=[SMEM] + [VMEM] * 4,
        out_specs=[VMEM] * steps,
        compiler_params=PARAMS,
        cost_estimate=cost(1),
        name="back_project",
    )(live, own_sens, other_sens, partial, other_partial)
    returned = [exchange(x, {0: s, 1: s ^ mirror}) for s, x in zip(order, grads)]

    far_ids = exchange(ids, {0: mirror})
    returned[0], passed_ids = lax.optimization_barrier((returned[0], swap_rows(far_ids)))
    other_returned = [swap_rows(x) for x in returned]

    total = jax.ShapeDtypeStruct((blocks, vecs, width), jnp.float32)
    own_sum = pl.pallas_call(
        functools.partial(sum_kernel, capacity),
        out_shape=total,
        in_specs=[SMEM] * 3 + [VMEM] * steps,
        out_specs=VMEM,
        compiler_params=PARAMS,
        cost_estimate=cost(1),
        name="sum_blocks",
    )(here, ids, passed_ids, *returned)
    return pl.pallas_call(
        functools.partial(finish_kernel, capacity),
        out_shape=total,
        in_specs=[SMEM] * 3 + [VMEM] * (1 + steps),
        out_specs=VMEM,
        compiler_params=PARAMS,
        cost_estimate=cost(1),
        name="finish_blocks",
    )(here, ids, far_ids, own_sum, *other_returned)


def solution(mesh):
    in_specs = (
        P(("parts", "tile"), None, None),
        P(("parts", "tile"), "row", None),
        P(("parts", "tile"), "row"),
        P(("parts", "tile"), None),
        P(("parts", "tile"), None),
    )
    out_specs = P(("parts", "tile"), None, None)
    return jax.shard_map(
        on_device, mesh=mesh, in_specs=in_specs, out_specs=out_specs, check_vma=False
    )
```

```python
import functools

import jax
import jax.numpy as jnp
from jax import lax
from jax.experimental import pallas as pl
from jax.experimental.pallas import tpu as pltpu
from jax.sharding import PartitionSpec as P

VMEM = pl.BlockSpec(memory_space=pltpu.VMEM)
SMEM = pl.BlockSpec(memory_space=pltpu.SMEM)
HBM = pl.BlockSpec(memory_space=pltpu.HBM)
ANY = pl.BlockSpec(memory_space=pl.ANY)
PARAMS = pltpu.CompilerParams(vmem_limit_bytes=32 << 20)


def swap_rows(x):
    return lax.ppermute(x, "row", [(0, 1), (1, 0)])


def exchange(x, apart):
    tiles = lax.axis_size("tile")
    pairs = [(2 * t + r, 2 * (t ^ apart[r]) + r) for t in range(tiles) for r in apart]
    return lax.ppermute(x, ("tile", "row"), pairs)


def in_hbm(x):
    return pltpu.with_memory_space_constraint(x, pltpu.HBM)


def cost(moved, flops=0):
    return pl.CostEstimate(flops=flops, bytes_accessed=moved, transcendentals=0)


def column_copies(slots, column_ref, sens_ref, out_ref, sems):
    width = out_ref.shape[1] // slots
    copies = []
    for slot in range(slots):
        start = pl.multiple_of(column_ref[slot] * width, 128)
        copies.append(
            pltpu.make_async_copy(
                sens_ref.at[:, pl.ds(start, width)],
                out_ref.at[:, pl.ds(slot * width, width)],
                sems.at[slot],
            )
        )
        copies[-1].start()
    return copies


def find_asked(list_ref, owner, blocks, slot, ids_ref):
    first, spare = owner * blocks, ids_ref.shape[0] - 1
    for k in range(list_ref.shape[1]):
        block = list_ref[0, k] - first
        mine = (block >= 0) & (block < blocks)
        ids_ref[jnp.where(mine, slot, spare)] = block
        slot = slot + mine.astype(jnp.int32)


def plan_kernel(tiles, capacity, blocks, here_ref, list_ref, mask_ref, sens_ref, *refs):
    column_ref, live_ref, own_ids_ref, out_ref = refs[:4]
    held_list_ref, held_mask_ref, count_ref, sems = refs[4:]
    steps = tiles // 2
    slots = steps * capacity
    pairs = [(list_ref, held_list_ref), (mask_ref, held_mask_ref)]
    copies = [pltpu.make_async_copy(*pair, sems.at[slots + i]) for i, pair in enumerate(pairs)]
    for copy in copies:
        copy.start()
    for s in range(tiles):
        count_ref[s] = 0
    for copy in copies:
        copy.wait()
    tile, core = here_ref[0], here_ref[1]
    mirror = tile ^ (tiles - 2)
    seen_from = jnp.where(core == 0, tile, mirror)
    for k in range(list_ref.shape[1]):
        apart = lax.div(held_list_ref[0, k], blocks) ^ seen_from
        count = count_ref[apart]
        count_ref[apart] = count + 1
        slot = (steps - 1 - apart) * capacity + count
        slot = jnp.where(apart < steps, slot, slots)
        column_ref[slot] = k
        live_ref[slot] = held_mask_ref[0, k]
    copies = column_copies(slots, column_ref, sens_ref, out_ref, sems)
    find_asked(held_list_ref, tile, blocks, 0, own_ids_ref)
    find_asked(held_list_ref, mirror, blocks, capacity, own_ids_ref)
    for copy in copies:
        copy.wait()


def stage_kernel(slots, column_ref, sens_ref, out_ref, sems):
    for copy in column_copies(slots, column_ref, sens_ref, out_ref, sems):
        copy.wait()


def search_kernel(tiles, capacity, blocks, here_ref, own_ids_ref, *refs):
    *lists, ids_ref = refs
    steps, tile = tiles // 2, here_ref[0]
    slots = steps * capacity
    for part, owner in enumerate((tile, tile ^ (tiles - 2))):
        for turn, list_ref in enumerate(lists):
            find_asked(list_ref, owner, blocks, part * slots + turn * capacity, ids_ref)
        for c in range(capacity):
            ids_ref[part * slots + (steps - 1) * capacity + c] = own_ids_ref[part * capacity + c]


def select_kernel(capacity, here_ref, ids_ref, own_ref, mirror_ref, *refs):
    *outs, dirs_ref, sem = refs
    core = here_ref[1]

    @pl.when(core == 0)
    def _():
        pltpu.make_async_copy(own_ref, dirs_ref, sem.at[0]).start()

    @pl.when(core != 0)
    def _():
        pltpu.make_async_copy(mirror_ref, dirs_ref, sem.at[0]).start()

    pltpu.make_async_copy(own_ref, dirs_ref, sem.at[0]).wait()
    start = core * (len(outs) * capacity)
    for turn, out_ref in enumerate(outs):
        for c in range(capacity):
            out_ref[c] = dirs_ref[ids_ref[start + turn * capacity + c]]


def predict_kernel(capacity, live_ref, own_ref, other_ref, weight_ref, *refs):
    *chunks, out_ref, flat_ref = refs
    vecs, width = chunks[0].shape[1:]
    for turn, chunk_ref in enumerate(chunks):
        for c in range(capacity):
            slot = turn * capacity + c
            live = live_ref[slot].astype(jnp.float32)
            block = chunk_ref[c].astype(jnp.float32) * live
            flat_ref[:, slot * width : (slot + 1) * width] = block.astype(jnp.bfloat16)
    weight = weight_ref[...]
    for side, sens_ref in enumerate((own_ref, other_ref)):
        product = lax.dot_general(
            sens_ref[...],
            flat_ref[...],
            (((1,), (1,)), ((), ())),
            preferred_element_type=jnp.float32,
        )
        out_ref[side, :vecs] = product.T
        out_ref[side, vecs:] = jnp.broadcast_to(weight * weight, (8, weight.shape[1]))


def back_kernel(capacity, live_ref, own_ref, other_ref, mine_ref, theirs_ref, *outs):
    vecs, width = outs[0].shape[1:]
    own = mine_ref[0, vecs : vecs + 1] * (mine_ref[0, :vecs] + theirs_ref[1, :vecs])
    other = theirs_ref[0, vecs : vecs + 1] * (mine_ref[1, :vecs] + theirs_ref[0, :vecs])
    own, other = own.astype(jnp.bfloat16), other.astype(jnp.bfloat16)
    for turn, out_ref in enumerate(outs):
        span = slice(turn * capacity * width, (turn + 1) * capacity * width)
        grads = jnp.dot(own, own_ref[:, span], preferred_element_type=jnp.float32)
        grads += jnp.dot(other, other_ref[:, span], preferred_element_type=jnp.float32)
        for c in range(capacity):
            live = live_ref[turn * capacity + c].astype(jnp.float32)
            part = grads[:, c * width : (c + 1) * width] * live
            out_ref[c] = part.astype(jnp.bfloat16)


def add_chunks(turns, capacity, places, chunks, out_ref):
    out_ref[...] = jnp.zeros_like(out_ref)
    for turn, chunk_ref in zip(turns, chunks):
        for c in range(capacity):
            out_ref[places(turn * capacity + c)] += chunk_ref[c].astype(jnp.float32)


def sum_kernel(turns, capacity, here_ref, near_ref, far_ref, *refs):
    *chunks, out_ref = refs
    core, slots = here_ref[1], len(chunks) * capacity
    add_chunks(
        turns,
        capacity,
        lambda slot: jnp.where(core == 0, near_ref[slot], far_ref[slots + slot]),
        chunks,
        out_ref,
    )


def finish_kernel(turns, capacity, here_ref, near_ref, far_ref, own_ref, *refs):
    *chunks, out_ref, total_ref, sems = refs
    core, slots = here_ref[1], len(chunks) * capacity
    add_chunks(
        turns,
        capacity,
        lambda slot: jnp.where(core == 0, far_ref[slots + slot], near_ref[slot]),
        chunks,
        total_ref,
    )
    parts = sems.shape[0]
    size = out_ref.shape[0] // parts
    copies = []
    for i in range(parts):
        span = pl.ds(i * size, size)
        total_ref[span] += own_ref[span]
        copies.append(pltpu.make_async_copy(total_ref.at[span], out_ref.at[span], sems.at[i]))
        copies[-1].start()
    for copy in copies:
        copy.wait()


def on_device(directions, sensitivity, data_weight, foot_list, foot_mask):
    tiles = lax.axis_size("tile")
    blocks, vecs, width = directions.shape
    rows = sensitivity.shape[1]
    foot = foot_list.shape[1]
    steps, capacity = tiles // 2, foot // tiles
    slots, mirror = steps * capacity, tiles - 2
    here = jnp.stack([lax.axis_index("tile"), lax.axis_index("row")]).astype(jnp.int32)
    order = list(reversed(range(steps)))

    own_sens = in_hbm(sensitivity[0])
    other_sens = in_hbm(swap_rows(sensitivity[0]))
    mirrored = exchange(directions, {1: mirror})
    lists = [exchange(foot_list, {0: s, 1: s}) for s in order[:-1]]

    table = jax.ShapeDtypeStruct((slots + 1,), jnp.int32)
    columns = pltpu.VMEM((rows, slots * width), jnp.bfloat16)
    column, live, own_ids, own_sens = pl.pallas_call(
        functools.partial(plan_kernel, tiles, capacity, blocks),
        out_shape=[table] * 2 + [jax.ShapeDtypeStruct((2 * capacity + 1,), jnp.int32), columns],
        in_specs=[SMEM] + [HBM] * 3,
        out_specs=[SMEM] * 3 + [VMEM],
        scratch_shapes=[
            pltpu.SMEM(foot_list.shape, jnp.int32),
            pltpu.SMEM(foot_mask.shape, jnp.int32),
            pltpu.SMEM((tiles,), jnp.int32),
            pltpu.SemaphoreType.DMA((slots + 2,)),
        ],
        compiler_params=PARAMS,
        cost_estimate=cost(1),
        name="plan_columns",
    )(here, in_hbm(foot_list), in_hbm(foot_mask), own_sens)

    chunk = jax.ShapeDtypeStruct((capacity, vecs, width), jnp.bfloat16)
    ids = pl.pallas_call(
        functools.partial(search_kernel, tiles, capacity, blocks),
        out_shape=jax.ShapeDtypeStruct((2 * slots + 1,), jnp.int32),
        in_specs=[SMEM] * (1 + steps),
        out_specs=SMEM,
        compiler_params=PARAMS,
        cost_estimate=cost(1),
        name="search_lists",
    )(here, own_ids, *lists)
    chunks = pl.pallas_call(
        functools.partial(select_kernel, capacity),
        out_shape=[chunk] * steps,
        in_specs=[SMEM] * 2 + [HBM, ANY],
        out_specs=[VMEM] * steps,
        scratch_shapes=[
            pltpu.VMEM(directions.shape, jnp.bfloat16),
            pltpu.SemaphoreType.DMA((1,)),
        ],
        compiler_params=PARAMS,
        cost_estimate=cost(1),
        name="select_blocks",
    )(here, ids, in_hbm(directions), mirrored)
    fetched = [exchange(x, {0: s, 1: s}) for s, x in zip(order[:-1], chunks)] + [chunks[-1]]

    other_sens = pl.pallas_call(
        functools.partial(stage_kernel, slots),
        out_shape=columns,
        in_specs=[SMEM, HBM],
        out_specs=VMEM,
        scratch_shapes=[pltpu.SemaphoreType.DMA((slots,))],
        compiler_params=PARAMS,
        cost_estimate=cost(1),
        name="stage_columns",
    )(column, other_sens)

    far_ids = exchange(ids, {0: mirror, 1: mirror})
    partial = pl.pallas_call(
        functools.partial(predict_kernel, capacity),
        out_shape=jax.ShapeDtypeStruct((2, vecs + 8, rows), jnp.float32),
        in_specs=[SMEM] + [VMEM] * (3 + steps),
        out_specs=VMEM,
        scratch_shapes=[pltpu.VMEM((vecs, slots * width), jnp.bfloat16)],
        compiler_params=PARAMS,
        cost_estimate=cost(1),
        name="predict",
    )(live, own_sens, other_sens, data_weight, *fetched)
    partial, far_ids = lax.optimization_barrier((partial, far_ids))
    other_partial = swap_rows(partial)

    grads = pl.pallas_call(
        functools.partial(back_kernel, capacity),
        out_shape=[chunk] * steps,
        in_specs=[SMEM] + [VMEM] * 4,
        out_specs=[VMEM] * steps,
        compiler_params=PARAMS,
        cost_estimate=cost(1),
        name="back_project",
    )(live, own_sens, other_sens, partial, other_partial)
    turns = list(range(0, steps, 2)) + list(range(1, steps, 2))
    returned = [exchange(grads[i], {0: order[i], 1: order[i] ^ mirror}) for i in turns]

    other_returned = [swap_rows(x) for x in returned]

    total = jax.ShapeDtypeStruct((blocks, vecs, width), jnp.float32)
    own_sum = pl.pallas_call(
        functools.partial(sum_kernel, turns, capacity),
        out_shape=total,
        in_specs=[SMEM] * 3 + [VMEM] * steps,
        out_specs=VMEM,
        compiler_params=PARAMS,
        cost_estimate=cost(1),
        name="sum_blocks",
    )(here, ids, far_ids, *returned)
    return pl.pallas_call(
        functools.partial(finish_kernel, turns, capacity),
        out_shape=total,
        in_specs=[SMEM] * 3 + [VMEM] * (1 + steps),
        out_specs=HBM,
        scratch_shapes=[
            pltpu.VMEM((blocks, vecs, width), jnp.float32),
            pltpu.SemaphoreType.DMA((4,)),
        ],
        compiler_params=PARAMS,
        cost_estimate=cost(1),
        name="finish_blocks",
    )(here, ids, far_ids, own_sum, *other_returned)


def solution(mesh):
    in_specs = (
        P(("parts", "tile"), None, None),
        P(("parts", "tile"), "row", None),
        P(("parts", "tile"), "row"),
        P(("parts", "tile"), None),
        P(("parts", "tile"), None),
    )
    out_specs = P(("parts", "tile"), None, None)
    return jax.shard_map(
        on_device, mesh=mesh, in_specs=in_specs, out_specs=out_specs, check_vma=False
    )
```

```python
import functools

import jax
import jax.numpy as jnp
from jax import lax
from jax.experimental import pallas as pl
from jax.experimental.pallas import tpu as pltpu
from jax.sharding import PartitionSpec as P

VMEM = pl.BlockSpec(memory_space=pltpu.VMEM)
SMEM = pl.BlockSpec(memory_space=pltpu.SMEM)
HBM = pl.BlockSpec(memory_space=pltpu.HBM)
ANY = pl.BlockSpec(memory_space=pl.ANY)
PARAMS = pltpu.CompilerParams(vmem_limit_bytes=32 << 20)


def swap_rows(x):
    return lax.ppermute(x, "row", [(0, 1), (1, 0)])


def exchange(x, apart):
    tiles = lax.axis_size("tile")
    pairs = [(2 * t + r, 2 * (t ^ apart[r]) + r) for t in range(tiles) for r in apart]
    return lax.ppermute(x, ("tile", "row"), pairs)


def in_hbm(x):
    return pltpu.with_memory_space_constraint(x, pltpu.HBM)


def cost(moved, flops=0):
    return pl.CostEstimate(flops=flops, bytes_accessed=moved, transcendentals=0)


def column_copies(slots, column_ref, sens_ref, out_ref, sems):
    width = out_ref.shape[1] // slots
    copies = []
    for slot in range(slots):
        start = pl.multiple_of(column_ref[slot] * width, 128)
        copies.append(
            pltpu.make_async_copy(
                sens_ref.at[:, pl.ds(start, width)],
                out_ref.at[:, pl.ds(slot * width, width)],
                sems.at[slot],
            )
        )
        copies[-1].start()
    return copies


def find_asked(list_ref, owner, blocks, slot, ids_ref):
    first, spare = owner * blocks, ids_ref.shape[0] - 1
    for k in range(list_ref.shape[1]):
        block = list_ref[0, k] - first
        mine = (block >= 0) & (block < blocks)
        ids_ref[jnp.where(mine, slot, spare)] = block
        slot = slot + mine.astype(jnp.int32)


def plan_kernel(tiles, capacity, blocks, here_ref, list_ref, mask_ref, sens_ref, *refs):
    column_ref, live_ref, own_ids_ref, out_ref = refs[:4]
    held_list_ref, held_mask_ref, count_ref, sems = refs[4:]
    steps = tiles // 2
    slots = steps * capacity
    pairs = [(list_ref, held_list_ref), (mask_ref, held_mask_ref)]
    copies = [pltpu.make_async_copy(*pair, sems.at[slots + i]) for i, pair in enumerate(pairs)]
    for copy in copies:
        copy.start()
    for s in range(tiles):
        count_ref[s] = 0
    for copy in copies:
        copy.wait()
    tile, core = here_ref[0], here_ref[1]
    mirror = tile ^ (tiles - 2)
    seen_from = jnp.where(core == 0, tile, mirror)
    for k in range(list_ref.shape[1]):
        apart = lax.div(held_list_ref[0, k], blocks) ^ seen_from
        count = count_ref[apart]
        count_ref[apart] = count + 1
        slot = (steps - 1 - apart) * capacity + count
        slot = jnp.where(apart < steps, slot, slots)
        column_ref[slot] = k
        live_ref[slot] = held_mask_ref[0, k]
    copies = column_copies(slots, column_ref, sens_ref, out_ref, sems)
    find_asked(held_list_ref, tile, blocks, 0, own_ids_ref)
    find_asked(held_list_ref, mirror, blocks, capacity, own_ids_ref)
    for copy in copies:
        copy.wait()


def stage_kernel(slots, column_ref, sens_ref, out_ref, sems):
    for copy in column_copies(slots, column_ref, sens_ref, out_ref, sems):
        copy.wait()


def search_kernel(tiles, capacity, blocks, here_ref, own_ids_ref, *refs):
    *lists, ids_ref = refs
    steps, tile = tiles // 2, here_ref[0]
    slots = steps * capacity
    for part, owner in enumerate((tile, tile ^ (tiles - 2))):
        for turn, list_ref in enumerate(lists):
            find_asked(list_ref, owner, blocks, part * slots + turn * capacity, ids_ref)
        for c in range(capacity):
            ids_ref[part * slots + (steps - 1) * capacity + c] = own_ids_ref[part * capacity + c]


def select_kernel(capacity, here_ref, ids_ref, own_ref, mirror_ref, *refs):
    *outs, dirs_ref, sem = refs
    core = here_ref[1]

    @pl.when(core == 0)
    def _():
        pltpu.make_async_copy(own_ref, dirs_ref, sem.at[0]).start()

    @pl.when(core != 0)
    def _():
        pltpu.make_async_copy(mirror_ref, dirs_ref, sem.at[0]).start()

    pltpu.make_async_copy(own_ref, dirs_ref, sem.at[0]).wait()
    start = core * (len(outs) * capacity)
    for turn, out_ref in enumerate(outs):
        for c in range(capacity):
            out_ref[c] = dirs_ref[ids_ref[start + turn * capacity + c]]


def predict_kernel(capacity, live_ref, own_ref, other_ref, weight_ref, *refs):
    *chunks, out_ref, flat_ref = refs
    vecs, width = chunks[0].shape[1:]
    for turn, chunk_ref in enumerate(chunks):
        for c in range(capacity):
            slot = turn * capacity + c
            live = live_ref[slot].astype(jnp.float32)
            block = chunk_ref[c].astype(jnp.float32) * live
            flat_ref[:, slot * width : (slot + 1) * width] = block.astype(jnp.bfloat16)
    weight = weight_ref[...]
    for side, sens_ref in enumerate((own_ref, other_ref)):
        product = lax.dot_general(
            sens_ref[...],
            flat_ref[...],
            (((1,), (1,)), ((), ())),
            preferred_element_type=jnp.float32,
        )
        out_ref[side, :vecs] = product.T
        out_ref[side, vecs:] = jnp.broadcast_to(weight * weight, (8, weight.shape[1]))


def back_kernel(capacity, live_ref, own_ref, other_ref, mine_ref, theirs_ref, *outs):
    vecs, width = outs[0].shape[1:]
    own = mine_ref[0, vecs : vecs + 1] * (mine_ref[0, :vecs] + theirs_ref[1, :vecs])
    other = theirs_ref[0, vecs : vecs + 1] * (mine_ref[1, :vecs] + theirs_ref[0, :vecs])
    own, other = own.astype(jnp.bfloat16), other.astype(jnp.bfloat16)
    for turn, out_ref in enumerate(outs):
        span = slice(turn * capacity * width, (turn + 1) * capacity * width)
        grads = jnp.dot(own, own_ref[:, span], preferred_element_type=jnp.float32)
        grads += jnp.dot(other, other_ref[:, span], preferred_element_type=jnp.float32)
        for c in range(capacity):
            live = live_ref[turn * capacity + c].astype(jnp.float32)
            part = grads[:, c * width : (c + 1) * width] * live
            out_ref[c] = part.astype(jnp.bfloat16)


def add_chunks(turns, capacity, places, kept, kept_ref, chunks, out_ref):
    out_ref[...] = jnp.zeros_like(out_ref)
    for turn, chunk_ref in zip(turns, chunks):
        for c in range(capacity):
            block = chunk_ref[c]
            if turn == len(turns) - 1:
                block = jnp.where(kept, kept_ref[c], block)
            out_ref[places(turn * capacity + c)] += block.astype(jnp.float32)


def sum_kernel(turns, capacity, here_ref, near_ref, far_ref, *refs):
    kept_ref, *chunks, out_ref = refs
    core, slots = here_ref[1], len(chunks) * capacity
    add_chunks(
        turns,
        capacity,
        lambda slot: jnp.where(core == 0, near_ref[slot], far_ref[slots + slot]),
        core == 0,
        kept_ref,
        chunks,
        out_ref,
    )


def finish_kernel(turns, capacity, here_ref, near_ref, far_ref, own_ref, *refs):
    kept_ref, *chunks, out_ref, total_ref, sems = refs
    core, slots = here_ref[1], len(chunks) * capacity
    add_chunks(
        turns,
        capacity,
        lambda slot: jnp.where(core == 0, far_ref[slots + slot], near_ref[slot]),
        core != 0,
        kept_ref,
        chunks,
        total_ref,
    )
    parts = sems.shape[0]
    size = out_ref.shape[0] // parts
    copies = []
    for i in range(parts):
        span = pl.ds(i * size, size)
        total_ref[span] += own_ref[span]
        copies.append(pltpu.make_async_copy(total_ref.at[span], out_ref.at[span], sems.at[i]))
        copies[-1].start()
    for copy in copies:
        copy.wait()


def on_device(directions, sensitivity, data_weight, foot_list, foot_mask):
    tiles = lax.axis_size("tile")
    blocks, vecs, width = directions.shape
    rows = sensitivity.shape[1]
    foot = foot_list.shape[1]
    steps, capacity = tiles // 2, foot // tiles
    slots, mirror = steps * capacity, tiles - 2
    here = jnp.stack([lax.axis_index("tile"), lax.axis_index("row")]).astype(jnp.int32)
    order = list(reversed(range(steps)))

    own_sens = in_hbm(sensitivity[0])
    other_sens = in_hbm(swap_rows(sensitivity[0]))
    mirrored = exchange(directions, {0: 1, 1: mirror})
    lists = [exchange(foot_list, {0: s, 1: s}) for s in order[:-1]]

    table = jax.ShapeDtypeStruct((slots + 1,), jnp.int32)
    columns = pltpu.VMEM((rows, slots * width), jnp.bfloat16)
    column, live, own_ids, own_sens = pl.pallas_call(
        functools.partial(plan_kernel, tiles, capacity, blocks),
        out_shape=[table] * 2 + [jax.ShapeDtypeStruct((2 * capacity + 1,), jnp.int32), columns],
        in_specs=[SMEM] + [HBM] * 3,
        out_specs=[SMEM] * 3 + [VMEM],
        scratch_shapes=[
            pltpu.SMEM(foot_list.shape, jnp.int32),
            pltpu.SMEM(foot_mask.shape, jnp.int32),
            pltpu.SMEM((tiles,), jnp.int32),
            pltpu.SemaphoreType.DMA((slots + 2,)),
        ],
        compiler_params=PARAMS,
        cost_estimate=cost(1),
        name="plan_columns",
    )(here, in_hbm(foot_list), in_hbm(foot_mask), own_sens)

    chunk = jax.ShapeDtypeStruct((capacity, vecs, width), jnp.bfloat16)
    ids = pl.pallas_call(
        functools.partial(search_kernel, tiles, capacity, blocks),
        out_shape=jax.ShapeDtypeStruct((2 * slots + 1,), jnp.int32),
        in_specs=[SMEM] * (1 + steps),
        out_specs=SMEM,
        compiler_params=PARAMS,
        cost_estimate=cost(1),
        name="search_lists",
    )(here, own_ids, *lists)
    chunks = pl.pallas_call(
        functools.partial(select_kernel, capacity),
        out_shape=[chunk] * steps,
        in_specs=[SMEM] * 2 + [HBM, ANY],
        out_specs=[VMEM] * steps,
        scratch_shapes=[
            pltpu.VMEM(directions.shape, jnp.bfloat16),
            pltpu.SemaphoreType.DMA((1,)),
        ],
        compiler_params=PARAMS,
        cost_estimate=cost(1),
        name="select_blocks",
    )(here, ids, in_hbm(directions), mirrored)
    fetched = [exchange(x, {0: s, 1: s}) for s, x in zip(order[:-1], chunks)] + [chunks[-1]]

    other_sens = pl.pallas_call(
        functools.partial(stage_kernel, slots),
        out_shape=columns,
        in_specs=[SMEM, HBM],
        out_specs=VMEM,
        scratch_shapes=[pltpu.SemaphoreType.DMA((slots,))],
        compiler_params=PARAMS,
        cost_estimate=cost(1),
        name="stage_columns",
    )(column, other_sens)

    far_ids = exchange(ids, {0: 1, 1: mirror})
    partial = pl.pallas_call(
        functools.partial(predict_kernel, capacity),
        out_shape=jax.ShapeDtypeStruct((2, vecs + 8, rows), jnp.float32),
        in_specs=[SMEM] + [VMEM] * (3 + steps),
        out_specs=VMEM,
        scratch_shapes=[pltpu.VMEM((vecs, slots * width), jnp.bfloat16)],
        compiler_params=PARAMS,
        cost_estimate=cost(1),
        name="predict",
    )(live, own_sens, other_sens, data_weight, *fetched)
    partial, far_ids = lax.optimization_barrier((partial, far_ids))
    other_partial = swap_rows(partial)

    grads = pl.pallas_call(
        functools.partial(back_kernel, capacity),
        out_shape=[chunk] * steps,
        in_specs=[SMEM] + [VMEM] * 4,
        out_specs=[VMEM] * steps,
        compiler_params=PARAMS,
        cost_estimate=cost(1),
        name="back_project",
    )(live, own_sens, other_sens, partial, other_partial)
    turns = list(range(steps))
    returned = [exchange(grads[i], {0: order[i] or 1, 1: order[i] ^ mirror}) for i in turns]
    own_grads = grads[steps - 1]
    returned[0], passed_ids = lax.optimization_barrier((returned[0], swap_rows(far_ids)))
    other_returned = [swap_rows(x) for x in returned]
    other_grads = swap_rows(own_grads)

    total = jax.ShapeDtypeStruct((blocks, vecs, width), jnp.float32)
    own_sum = pl.pallas_call(
        functools.partial(sum_kernel, turns, capacity),
        out_shape=total,
        in_specs=[SMEM] * 3 + [VMEM] * (1 + steps),
        out_specs=VMEM,
        compiler_params=PARAMS,
        cost_estimate=cost(1),
        name="sum_blocks",
    )(here, ids, far_ids, own_grads, *returned)
    return pl.pallas_call(
        functools.partial(finish_kernel, turns, capacity),
        out_shape=total,
        in_specs=[SMEM] * 3 + [VMEM] * (2 + steps),
        out_specs=HBM,
        scratch_shapes=[
            pltpu.VMEM((blocks, vecs, width), jnp.float32),
            pltpu.SemaphoreType.DMA((4,)),
        ],
        compiler_params=PARAMS,
        cost_estimate=cost(1),
        name="finish_blocks",
    )(here, ids, passed_ids, own_sum, other_grads, *other_returned)


def solution(mesh):
    in_specs = (
        P(("parts", "tile"), None, None),
        P(("parts", "tile"), "row", None),
        P(("parts", "tile"), "row"),
        P(("parts", "tile"), None),
        P(("parts", "tile"), None),
    )
    out_specs = P(("parts", "tile"), None, None)
    return jax.shard_map(
        on_device, mesh=mesh, in_specs=in_specs, out_specs=out_specs, check_vma=False
    )
```

```python
import functools

import jax
import jax.numpy as jnp
from jax import lax
from jax.experimental import pallas as pl
from jax.experimental.pallas import tpu as pltpu
from jax.sharding import PartitionSpec as P

VMEM = pl.BlockSpec(memory_space=pltpu.VMEM)
SMEM = pl.BlockSpec(memory_space=pltpu.SMEM)
HBM = pl.BlockSpec(memory_space=pltpu.HBM)
ANY = pl.BlockSpec(memory_space=pl.ANY)
PARAMS = pltpu.CompilerParams(vmem_limit_bytes=32 << 20)


def swap_rows(x):
    return lax.ppermute(x, "row", [(0, 1), (1, 0)])


def exchange(x, apart):
    tiles = lax.axis_size("tile")
    pairs = [(2 * t + r, 2 * (t ^ apart[r]) + r) for t in range(tiles) for r in apart]
    return lax.ppermute(x, ("tile", "row"), pairs)


def in_hbm(x):
    return pltpu.with_memory_space_constraint(x, pltpu.HBM)


def cost(moved, flops=0):
    return pl.CostEstimate(flops=flops, bytes_accessed=moved, transcendentals=0)


def column_copies(slots, column_ref, sens_ref, out_ref, sems):
    width = out_ref.shape[1] // slots
    copies = []
    for slot in range(slots):
        start = pl.multiple_of(column_ref[slot] * width, 128)
        copies.append(
            pltpu.make_async_copy(
                sens_ref.at[:, pl.ds(start, width)],
                out_ref.at[:, pl.ds(slot * width, width)],
                sems.at[slot],
            )
        )
        copies[-1].start()
    return copies


def find_asked(list_ref, owner, blocks, slot, ids_ref):
    first, spare = owner * blocks, ids_ref.shape[0] - 1
    for k in range(list_ref.shape[1]):
        block = list_ref[0, k] - first
        mine = (block >= 0) & (block < blocks)
        ids_ref[jnp.where(mine, slot, spare)] = block
        slot = slot + mine.astype(jnp.int32)


def plan_kernel(tiles, capacity, blocks, here_ref, list_ref, mask_ref, sens_ref, *refs):
    column_ref, live_ref, own_ids_ref, out_ref = refs[:4]
    held_list_ref, held_mask_ref, count_ref, sems = refs[4:]
    steps = tiles // 2
    slots = steps * capacity
    pairs = [(list_ref, held_list_ref), (mask_ref, held_mask_ref)]
    copies = [pltpu.make_async_copy(*pair, sems.at[slots + i]) for i, pair in enumerate(pairs)]
    for copy in copies:
        copy.start()
    for s in range(tiles):
        count_ref[s] = 0
    for copy in copies:
        copy.wait()
    tile, core = here_ref[0], here_ref[1]
    mirror = tile ^ (tiles - 2)
    seen_from = jnp.where(core == 0, tile, mirror)
    for k in range(list_ref.shape[1]):
        apart = lax.div(held_list_ref[0, k], blocks) ^ seen_from
        count = count_ref[apart]
        count_ref[apart] = count + 1
        slot = (steps - 1 - apart) * capacity + count
        slot = jnp.where(apart < steps, slot, slots)
        column_ref[slot] = k
        live_ref[slot] = held_mask_ref[0, k]
    copies = column_copies(slots, column_ref, sens_ref, out_ref, sems)
    find_asked(held_list_ref, tile, blocks, 0, own_ids_ref)
    find_asked(held_list_ref, mirror, blocks, capacity, own_ids_ref)
    for copy in copies:
        copy.wait()


def search_lists(owner, part, capacity, blocks, own_ids_ref, lists, ids_ref):
    for turn, list_ref in enumerate(lists):
        find_asked(list_ref, owner, blocks, turn * capacity, ids_ref)
    for c in range(capacity):
        ids_ref[len(lists) * capacity + c] = own_ids_ref[part * capacity + c]


def stage_kernel(tiles, capacity, blocks, here_ref, own_ids_ref, column_ref, *refs):
    *lists, sens_ref, out_ref, near_ref, sems = refs
    copies = column_copies(tiles // 2 * capacity, column_ref, sens_ref, out_ref, sems)
    search_lists(here_ref[0], 0, capacity, blocks, own_ids_ref, lists, near_ref)
    for copy in copies:
        copy.wait()


def search_kernel(tiles, capacity, blocks, here_ref, own_ids_ref, *refs):
    *lists, ids_ref = refs
    core = here_ref[1]
    owner = jnp.where(core == 0, here_ref[0], here_ref[0] ^ (tiles - 2))
    search_lists(owner, core, capacity, blocks, own_ids_ref, lists, ids_ref)


def select_kernel(capacity, here_ref, ids_ref, own_ref, mirror_ref, *refs):
    *outs, dirs_ref, sem = refs
    core = here_ref[1]

    @pl.when(core == 0)
    def _():
        pltpu.make_async_copy(own_ref, dirs_ref, sem.at[0]).start()

    @pl.when(core != 0)
    def _():
        pltpu.make_async_copy(mirror_ref, dirs_ref, sem.at[0]).start()

    pltpu.make_async_copy(own_ref, dirs_ref, sem.at[0]).wait()
    for turn, out_ref in enumerate(outs):
        for c in range(capacity):
            out_ref[c] = dirs_ref[ids_ref[turn * capacity + c]]


def predict_kernel(capacity, live_ref, own_ref, other_ref, weight_ref, *refs):
    *chunks, out_ref, flat_ref = refs
    vecs, width = chunks[0].shape[1:]
    for turn, chunk_ref in enumerate(chunks):
        for c in range(capacity):
            slot = turn * capacity + c
            live = live_ref[slot].astype(jnp.float32)
            block = chunk_ref[c].astype(jnp.float32) * live
            flat_ref[:, slot * width : (slot + 1) * width] = block.astype(jnp.bfloat16)
    weight = weight_ref[...]
    for side, sens_ref in enumerate((own_ref, other_ref)):
        product = lax.dot_general(
            sens_ref[...],
            flat_ref[...],
            (((1,), (1,)), ((), ())),
            preferred_element_type=jnp.float32,
        )
        out_ref[side, :vecs] = product.T
        out_ref[side, vecs:] = jnp.broadcast_to(weight * weight, (8, weight.shape[1]))


def back_kernel(capacity, live_ref, own_ref, other_ref, mine_ref, theirs_ref, *outs):
    vecs, width = outs[0].shape[1:]
    own = mine_ref[0, vecs : vecs + 1] * (mine_ref[0, :vecs] + theirs_ref[1, :vecs])
    other = theirs_ref[0, vecs : vecs + 1] * (mine_ref[1, :vecs] + theirs_ref[0, :vecs])
    own, other = own.astype(jnp.bfloat16), other.astype(jnp.bfloat16)
    for turn, out_ref in enumerate(outs):
        span = slice(turn * capacity * width, (turn + 1) * capacity * width)
        grads = jnp.dot(own, own_ref[:, span], preferred_element_type=jnp.float32)
        grads += jnp.dot(other, other_ref[:, span], preferred_element_type=jnp.float32)
        for c in range(capacity):
            live = live_ref[turn * capacity + c].astype(jnp.float32)
            part = grads[:, c * width : (c + 1) * width] * live
            out_ref[c] = part.astype(jnp.bfloat16)


def add_chunks(turns, capacity, places, kept, kept_ref, chunks, out_ref):
    out_ref[...] = jnp.zeros_like(out_ref)
    for turn, chunk_ref in zip(turns, chunks):
        for c in range(capacity):
            block = chunk_ref[c]
            if turn == len(turns) - 1:
                block = jnp.where(kept, kept_ref[c], block)
            out_ref[places(turn * capacity + c)] += block.astype(jnp.float32)


def sum_kernel(turns, capacity, here_ref, near_ref, far_ref, *refs):
    kept_ref, *chunks, out_ref = refs
    core = here_ref[1]
    add_chunks(
        turns,
        capacity,
        lambda slot: jnp.where(core == 0, near_ref[slot], far_ref[slot]),
        core == 0,
        kept_ref,
        chunks,
        out_ref,
    )


def finish_kernel(turns, capacity, here_ref, near_ref, far_ref, own_ref, *refs):
    kept_ref, *chunks, out_ref, total_ref, sems = refs
    core = here_ref[1]
    add_chunks(
        turns,
        capacity,
        lambda slot: jnp.where(core == 0, far_ref[slot], near_ref[slot]),
        core != 0,
        kept_ref,
        chunks,
        total_ref,
    )
    parts = sems.shape[0]
    size = out_ref.shape[0] // parts
    copies = []
    for i in range(parts):
        span = pl.ds(i * size, size)
        total_ref[span] += own_ref[span]
        copies.append(pltpu.make_async_copy(total_ref.at[span], out_ref.at[span], sems.at[i]))
        copies[-1].start()
    for copy in copies:
        copy.wait()


def on_device(directions, sensitivity, data_weight, foot_list, foot_mask):
    tiles = lax.axis_size("tile")
    blocks, vecs, width = directions.shape
    rows = sensitivity.shape[1]
    foot = foot_list.shape[1]
    steps, capacity = tiles // 2, foot // tiles
    slots, mirror = steps * capacity, tiles - 2
    here = jnp.stack([lax.axis_index("tile"), lax.axis_index("row")]).astype(jnp.int32)
    order = list(reversed(range(steps)))

    own_sens = in_hbm(sensitivity[0])
    other_sens = in_hbm(swap_rows(sensitivity[0]))
    mirrored = exchange(directions, {0: 1, 1: mirror})
    lists = [exchange(foot_list, {0: s, 1: s}) for s in order[:-1]]

    table = jax.ShapeDtypeStruct((slots + 1,), jnp.int32)
    columns = pltpu.VMEM((rows, slots * width), jnp.bfloat16)
    column, live, own_ids, own_sens = pl.pallas_call(
        functools.partial(plan_kernel, tiles, capacity, blocks),
        out_shape=[table] * 2 + [jax.ShapeDtypeStruct((2 * capacity + 1,), jnp.int32), columns],
        in_specs=[SMEM] + [HBM] * 3,
        out_specs=[SMEM] * 3 + [VMEM],
        scratch_shapes=[
            pltpu.SMEM(foot_list.shape, jnp.int32),
            pltpu.SMEM(foot_mask.shape, jnp.int32),
            pltpu.SMEM((tiles,), jnp.int32),
            pltpu.SemaphoreType.DMA((slots + 2,)),
        ],
        compiler_params=PARAMS,
        cost_estimate=cost(1),
        name="plan_columns",
    )(here, in_hbm(foot_list), in_hbm(foot_mask), own_sens)

    chunk = jax.ShapeDtypeStruct((capacity, vecs, width), jnp.bfloat16)
    ids = pl.pallas_call(
        functools.partial(search_kernel, tiles, capacity, blocks),
        out_shape=table,
        in_specs=[SMEM] * (1 + steps),
        out_specs=SMEM,
        compiler_params=PARAMS,
        cost_estimate=cost(1),
        name="search_lists",
    )(here, own_ids, *lists)
    chunks = pl.pallas_call(
        functools.partial(select_kernel, capacity),
        out_shape=[chunk] * steps,
        in_specs=[SMEM] * 2 + [HBM, ANY],
        out_specs=[VMEM] * steps,
        scratch_shapes=[
            pltpu.VMEM(directions.shape, jnp.bfloat16),
            pltpu.SemaphoreType.DMA((1,)),
        ],
        compiler_params=PARAMS,
        cost_estimate=cost(1),
        name="select_blocks",
    )(here, ids, in_hbm(directions), mirrored)
    fetched = [exchange(x, {0: s, 1: s}) for s, x in zip(order[:-1], chunks)] + [chunks[-1]]

    other_sens, near_ids = pl.pallas_call(
        functools.partial(stage_kernel, tiles, capacity, blocks),
        out_shape=[columns, table],
        in_specs=[SMEM] * (2 + steps) + [HBM],
        out_specs=[VMEM, SMEM],
        scratch_shapes=[pltpu.SemaphoreType.DMA((slots,))],
        compiler_params=PARAMS,
        cost_estimate=cost(1),
        name="stage_columns",
    )(here, own_ids, column, *lists, other_sens)

    far_ids = exchange(ids, {0: 1, 1: mirror})
    partial = pl.pallas_call(
        functools.partial(predict_kernel, capacity),
        out_shape=jax.ShapeDtypeStruct((2, vecs + 8, rows), jnp.float32),
        in_specs=[SMEM] + [VMEM] * (3 + steps),
        out_specs=VMEM,
        scratch_shapes=[pltpu.VMEM((vecs, slots * width), jnp.bfloat16)],
        compiler_params=PARAMS,
        cost_estimate=cost(1),
        name="predict",
    )(live, own_sens, other_sens, data_weight, *fetched)
    partial, far_ids = lax.optimization_barrier((partial, far_ids))
    other_partial = swap_rows(partial)

    grads = pl.pallas_call(
        functools.partial(back_kernel, capacity),
        out_shape=[chunk] * steps,
        in_specs=[SMEM] + [VMEM] * 4,
        out_specs=[VMEM] * steps,
        compiler_params=PARAMS,
        cost_estimate=cost(1),
        name="back_project",
    )(live, own_sens, other_sens, partial, other_partial)
    turns = list(range(steps))
    returned = [exchange(grads[i], {0: order[i] or 1, 1: order[i] ^ mirror}) for i in turns]
    own_grads = grads[steps - 1]
    returned[0], passed_ids = lax.optimization_barrier((returned[0], swap_rows(far_ids)))
    other_returned = [swap_rows(x) for x in returned]
    other_grads = swap_rows(own_grads)

    total = jax.ShapeDtypeStruct((blocks, vecs, width), jnp.float32)
    own_sum = pl.pallas_call(
        functools.partial(sum_kernel, turns, capacity),
        out_shape=total,
        in_specs=[SMEM] * 3 + [VMEM] * (1 + steps),
        out_specs=VMEM,
        compiler_params=PARAMS,
        cost_estimate=cost(1),
        name="sum_blocks",
    )(here, near_ids, far_ids, own_grads, *returned)
    return pl.pallas_call(
        functools.partial(finish_kernel, turns, capacity),
        out_shape=total,
        in_specs=[SMEM] * 3 + [VMEM] * (2 + steps),
        out_specs=HBM,
        scratch_shapes=[
            pltpu.VMEM((blocks, vecs, width), jnp.float32),
            pltpu.SemaphoreType.DMA((4,)),
        ],
        compiler_params=PARAMS,
        cost_estimate=cost(1),
        name="finish_blocks",
    )(here, near_ids, passed_ids, own_sum, other_grads, *other_returned)


def solution(mesh):
    in_specs = (
        P(("parts", "tile"), None, None),
        P(("parts", "tile"), "row", None),
        P(("parts", "tile"), "row"),
        P(("parts", "tile"), None),
        P(("parts", "tile"), None),
    )
    out_specs = P(("parts", "tile"), None, None)
    return jax.shard_map(
        on_device, mesh=mesh, in_specs=in_specs, out_specs=out_specs, check_vma=False
    )
```

```python
import functools

import jax
import jax.numpy as jnp
from jax import lax
from jax.experimental import pallas as pl
from jax.experimental.pallas import tpu as pltpu
from jax.sharding import PartitionSpec as P

VMEM = pl.BlockSpec(memory_space=pltpu.VMEM)
SMEM = pl.BlockSpec(memory_space=pltpu.SMEM)
HBM = pl.BlockSpec(memory_space=pltpu.HBM)
ANY = pl.BlockSpec(memory_space=pl.ANY)
PARAMS = pltpu.CompilerParams(vmem_limit_bytes=32 << 20)


def swap_rows(x):
    return lax.ppermute(x, "row", [(0, 1), (1, 0)])


def exchange(x, apart):
    tiles = lax.axis_size("tile")
    pairs = [(2 * t + r, 2 * (t ^ apart[r]) + r) for t in range(tiles) for r in apart]
    return lax.ppermute(x, ("tile", "row"), pairs)


def in_hbm(x):
    return pltpu.with_memory_space_constraint(x, pltpu.HBM)


def cost(moved, flops=0):
    return pl.CostEstimate(flops=flops, bytes_accessed=moved, transcendentals=0)


def column_copies(slots, column_ref, sens_ref, out_ref, sems):
    width = out_ref.shape[1] // slots
    copies = []
    for slot in range(slots):
        start = pl.multiple_of(column_ref[slot] * width, 128)
        copies.append(
            pltpu.make_async_copy(
                sens_ref.at[:, pl.ds(start, width)],
                out_ref.at[:, pl.ds(slot * width, width)],
                sems.at[slot],
            )
        )
        copies[-1].start()
    return copies


def find_asked(list_ref, owner, blocks, slot, ids_ref):
    first, spare = owner * blocks, ids_ref.shape[0] - 1
    for k in range(list_ref.shape[1]):
        block = list_ref[0, k] - first
        mine = (block >= 0) & (block < blocks)
        ids_ref[jnp.where(mine, slot, spare)] = block
        slot = slot + mine.astype(jnp.int32)


def plan_kernel(tiles, capacity, blocks, here_ref, list_ref, mask_ref, sens_ref, *refs):
    column_ref, live_ref, own_ids_ref, out_ref = refs[:4]
    held_list_ref, held_mask_ref, count_ref, sems = refs[4:]
    steps = tiles // 2
    slots = steps * capacity
    pairs = [(list_ref, held_list_ref), (mask_ref, held_mask_ref)]
    copies = [pltpu.make_async_copy(*pair, sems.at[slots + i]) for i, pair in enumerate(pairs)]
    for copy in copies:
        copy.start()
    for s in range(tiles):
        count_ref[s] = 0
    for copy in copies:
        copy.wait()
    tile, core = here_ref[0], here_ref[1]
    mirror = tile ^ (tiles - 2)
    seen_from = jnp.where(core == 0, tile, mirror)
    for k in range(list_ref.shape[1]):
        apart = lax.div(held_list_ref[0, k], blocks) ^ seen_from
        count = count_ref[apart]
        count_ref[apart] = count + 1
        slot = (steps - 1 - apart) * capacity + count
        slot = jnp.where(apart < steps, slot, slots)
        column_ref[slot] = k
        live_ref[slot] = held_mask_ref[0, k]
    copies = column_copies(slots, column_ref, sens_ref, out_ref, sems)
    find_asked(held_list_ref, tile, blocks, 0, own_ids_ref)
    find_asked(held_list_ref, mirror, blocks, capacity, own_ids_ref)
    for copy in copies:
        copy.wait()


def search_lists(owner, part, capacity, blocks, own_ids_ref, lists, ids_ref):
    for turn, list_ref in enumerate(lists):
        find_asked(list_ref, owner, blocks, turn * capacity, ids_ref)
    for c in range(capacity):
        ids_ref[len(lists) * capacity + c] = own_ids_ref[part * capacity + c]


def stage_kernel(tiles, capacity, blocks, here_ref, own_ids_ref, column_ref, *refs):
    *lists, sens_ref, out_ref, near_ref, sems = refs
    copies = column_copies(tiles // 2 * capacity, column_ref, sens_ref, out_ref, sems)
    search_lists(here_ref[0], 0, capacity, blocks, own_ids_ref, lists, near_ref)
    for copy in copies:
        copy.wait()


def search_kernel(tiles, capacity, blocks, here_ref, own_ids_ref, *refs):
    *lists, ids_ref = refs
    core = here_ref[1]
    owner = jnp.where(core == 0, here_ref[0], here_ref[0] ^ (tiles - 2))
    search_lists(owner, core, capacity, blocks, own_ids_ref, lists, ids_ref)


def select_kernel(capacity, here_ref, ids_ref, own_ref, mirror_ref, *refs):
    *outs, dirs_ref, sem = refs
    core = here_ref[1]

    @pl.when(core == 0)
    def _():
        pltpu.make_async_copy(own_ref, dirs_ref, sem.at[0]).start()

    @pl.when(core != 0)
    def _():
        pltpu.make_async_copy(mirror_ref, dirs_ref, sem.at[0]).start()

    pltpu.make_async_copy(own_ref, dirs_ref, sem.at[0]).wait()
    for turn, out_ref in enumerate(outs):
        for c in range(capacity):
            out_ref[c] = dirs_ref[ids_ref[turn * capacity + c]]


def predict_kernel(turns, capacity, live_ref, own_ref, other_ref, weight_ref, *refs):
    *chunks, out_ref, flat_ref = refs
    vecs, width = chunks[0].shape[1:]
    for turn, chunk_ref in zip(turns, chunks):
        for c in range(capacity):
            slot = turn * capacity + c
            live = live_ref[slot].astype(jnp.float32)
            block = chunk_ref[c].astype(jnp.float32) * live
            flat_ref[:, slot * width : (slot + 1) * width] = block.astype(jnp.bfloat16)
    weight = weight_ref[...]
    for side, sens_ref in enumerate((own_ref, other_ref)):
        product = lax.dot_general(
            sens_ref[...],
            flat_ref[...],
            (((1,), (1,)), ((), ())),
            preferred_element_type=jnp.float32,
        )
        out_ref[side, :vecs] = product.T
        out_ref[side, vecs:] = jnp.broadcast_to(weight * weight, (8, weight.shape[1]))


def back_kernel(capacity, live_ref, own_ref, other_ref, mine_ref, theirs_ref, *outs):
    vecs, width = outs[0].shape[1:]
    own = mine_ref[0, vecs : vecs + 1] * (mine_ref[0, :vecs] + theirs_ref[1, :vecs])
    other = theirs_ref[0, vecs : vecs + 1] * (mine_ref[1, :vecs] + theirs_ref[0, :vecs])
    own, other = own.astype(jnp.bfloat16), other.astype(jnp.bfloat16)
    for turn, out_ref in enumerate(outs):
        span = slice(turn * capacity * width, (turn + 1) * capacity * width)
        grads = jnp.dot(own, own_ref[:, span], preferred_element_type=jnp.float32)
        grads += jnp.dot(other, other_ref[:, span], preferred_element_type=jnp.float32)
        for c in range(capacity):
            live = live_ref[turn * capacity + c].astype(jnp.float32)
            part = grads[:, c * width : (c + 1) * width] * live
            out_ref[c] = part.astype(jnp.bfloat16)


def add_chunks(turns, capacity, places, kept, kept_ref, chunks, out_ref):
    out_ref[...] = jnp.zeros_like(out_ref)
    for turn, chunk_ref in zip(turns, chunks):
        for c in range(capacity):
            block = chunk_ref[c]
            if turn == len(turns) - 1:
                block = jnp.where(kept, kept_ref[c], block)
            out_ref[places(turn * capacity + c)] += block.astype(jnp.float32)


def sum_kernel(turns, capacity, here_ref, near_ref, far_ref, *refs):
    kept_ref, *chunks, out_ref = refs
    core = here_ref[1]
    add_chunks(
        turns,
        capacity,
        lambda slot: jnp.where(core == 0, near_ref[slot], far_ref[slot]),
        core == 0,
        kept_ref,
        chunks,
        out_ref,
    )


def finish_kernel(turns, capacity, here_ref, near_ref, far_ref, own_ref, *refs):
    kept_ref, *chunks, out_ref, total_ref, sems = refs
    core = here_ref[1]
    add_chunks(
        turns,
        capacity,
        lambda slot: jnp.where(core == 0, far_ref[slot], near_ref[slot]),
        core != 0,
        kept_ref,
        chunks,
        total_ref,
    )
    parts = sems.shape[0]
    size = out_ref.shape[0] // parts
    copies = []
    for i in range(parts):
        span = pl.ds(i * size, size)
        total_ref[span] += own_ref[span]
        copies.append(pltpu.make_async_copy(total_ref.at[span], out_ref.at[span], sems.at[i]))
        copies[-1].start()
    for copy in copies:
        copy.wait()


def on_device(directions, sensitivity, data_weight, foot_list, foot_mask):
    tiles = lax.axis_size("tile")
    blocks, vecs, width = directions.shape
    rows = sensitivity.shape[1]
    foot = foot_list.shape[1]
    steps, capacity = tiles // 2, foot // tiles
    slots, mirror = steps * capacity, tiles - 2
    here = jnp.stack([lax.axis_index("tile"), lax.axis_index("row")]).astype(jnp.int32)
    order = list(reversed(range(steps)))
    came = [0] + list(range(steps - 2, 0, -1)) + [steps - 1]

    own_sens = in_hbm(sensitivity[0])
    other_sens = in_hbm(swap_rows(sensitivity[0]))
    mirrored = exchange(directions, {0: 1, 1: mirror})
    lists = [exchange(foot_list, {0: s, 1: s}) for s in order[:-1]]

    table = jax.ShapeDtypeStruct((slots + 1,), jnp.int32)
    columns = pltpu.VMEM((rows, slots * width), jnp.bfloat16)
    column, live, own_ids, own_sens = pl.pallas_call(
        functools.partial(plan_kernel, tiles, capacity, blocks),
        out_shape=[table] * 2 + [jax.ShapeDtypeStruct((2 * capacity + 1,), jnp.int32), columns],
        in_specs=[SMEM] + [HBM] * 3,
        out_specs=[SMEM] * 3 + [VMEM],
        scratch_shapes=[
            pltpu.SMEM(foot_list.shape, jnp.int32),
            pltpu.SMEM(foot_mask.shape, jnp.int32),
            pltpu.SMEM((tiles,), jnp.int32),
            pltpu.SemaphoreType.DMA((slots + 2,)),
        ],
        compiler_params=PARAMS,
        cost_estimate=cost(1),
        name="plan_columns",
    )(here, in_hbm(foot_list), in_hbm(foot_mask), own_sens)

    chunk = jax.ShapeDtypeStruct((capacity, vecs, width), jnp.bfloat16)
    ids = pl.pallas_call(
        functools.partial(search_kernel, tiles, capacity, blocks),
        out_shape=table,
        in_specs=[SMEM] * (1 + steps),
        out_specs=SMEM,
        compiler_params=PARAMS,
        cost_estimate=cost(1),
        name="search_lists",
    )(here, own_ids, *lists)
    chunks = pl.pallas_call(
        functools.partial(select_kernel, capacity),
        out_shape=[chunk] * steps,
        in_specs=[SMEM] * 2 + [HBM, ANY],
        out_specs=[VMEM] * steps,
        scratch_shapes=[
            pltpu.VMEM(directions.shape, jnp.bfloat16),
            pltpu.SemaphoreType.DMA((1,)),
        ],
        compiler_params=PARAMS,
        cost_estimate=cost(1),
        name="select_blocks",
    )(here, ids, in_hbm(directions), mirrored)
    fetched = [exchange(x, {0: s, 1: s}) for s, x in zip(order[:-1], chunks)] + [chunks[-1]]

    other_sens, near_ids = pl.pallas_call(
        functools.partial(stage_kernel, tiles, capacity, blocks),
        out_shape=[columns, table],
        in_specs=[SMEM] * (2 + steps) + [HBM],
        out_specs=[VMEM, SMEM],
        scratch_shapes=[pltpu.SemaphoreType.DMA((slots,))],
        compiler_params=PARAMS,
        cost_estimate=cost(1),
        name="stage_columns",
    )(here, own_ids, column, *lists, other_sens)

    far_ids = exchange(ids, {0: 1, 1: mirror})
    partial = pl.pallas_call(
        functools.partial(predict_kernel, came, capacity),
        out_shape=jax.ShapeDtypeStruct((2, vecs + 8, rows), jnp.float32),
        in_specs=[SMEM] + [VMEM] * (3 + steps),
        out_specs=VMEM,
        scratch_shapes=[pltpu.VMEM((vecs, slots * width), jnp.bfloat16)],
        compiler_params=PARAMS,
        cost_estimate=cost(1),
        name="predict",
    )(live, own_sens, other_sens, data_weight, *[fetched[i] for i in came])
    partial, far_ids = lax.optimization_barrier((partial, far_ids))
    other_partial = swap_rows(partial)

    grads = pl.pallas_call(
        functools.partial(back_kernel, capacity),
        out_shape=[chunk] * steps,
        in_specs=[SMEM] + [VMEM] * 4,
        out_specs=[VMEM] * steps,
        compiler_params=PARAMS,
        cost_estimate=cost(1),
        name="back_project",
    )(live, own_sens, other_sens, partial, other_partial)
    turns = list(range(steps))
    returned = [exchange(grads[i], {0: order[i] or 1, 1: order[i] ^ mirror}) for i in turns]
    own_grads = grads[steps - 1]
    returned[0], passed_ids = lax.optimization_barrier((returned[0], swap_rows(far_ids)))
    other_returned = [swap_rows(x) for x in returned]
    other_grads = swap_rows(own_grads)

    total = jax.ShapeDtypeStruct((blocks, vecs, width), jnp.float32)
    own_sum = pl.pallas_call(
        functools.partial(sum_kernel, turns, capacity),
        out_shape=total,
        in_specs=[SMEM] * 3 + [VMEM] * (1 + steps),
        out_specs=VMEM,
        compiler_params=PARAMS,
        cost_estimate=cost(1),
        name="sum_blocks",
    )(here, near_ids, far_ids, own_grads, *returned)
    return pl.pallas_call(
        functools.partial(finish_kernel, turns, capacity),
        out_shape=total,
        in_specs=[SMEM] * 3 + [VMEM] * (2 + steps),
        out_specs=HBM,
        scratch_shapes=[
            pltpu.VMEM((blocks, vecs, width), jnp.float32),
            pltpu.SemaphoreType.DMA((4,)),
        ],
        compiler_params=PARAMS,
        cost_estimate=cost(1),
        name="finish_blocks",
    )(here, near_ids, passed_ids, own_sum, other_grads, *other_returned)


def solution(mesh):
    in_specs = (
        P(("parts", "tile"), None, None),
        P(("parts", "tile"), "row", None),
        P(("parts", "tile"), "row"),
        P(("parts", "tile"), None),
        P(("parts", "tile"), None),
    )
    out_specs = P(("parts", "tile"), None, None)
    return jax.shard_map(
        on_device, mesh=mesh, in_specs=in_specs, out_specs=out_specs, check_vma=False
    )
```
